32 devices in a mesh: row: 4 (over y, core), col: 8 (over z, x).
Axes of the slice: x: 2, y: 2, z: 4, core: 2. Of those that a mesh axis runs over, the one named last changes fastest.
Arguments:
- blocks: float32 [32, 8, 256, 256], P('row', 'col'), may hold values from -6 to 6
- panel_rows: int32 [2, 16], P(None, 'row'), may hold values from -1 to 191, as said below
- target_slots: int32 [2, 32, 8], P(None, 'row', 'col'), may hold values from -1 to 3, as said below
- diag_inverse: float32 [2, 256, 256], replicated, may hold values from -1 to 1, as said below
- cross_block: float32 [256, 256], replicated, may hold values from -6 to 6
Outputs:
- factored: float32 [32, 8, 256, 256], P('row', 'col')
The draws below stay inside these ranges and needn't reach their ends.
Inputs may be any that keep to these rules, and one draw needn't show every extreme that they name: `panel_rows`: slot q * 2 + m of row device r stands for the m-th structure row of block column class r + q times the number of row devices; both lists are -1 where that class is 0 or 1, and list 0 is -1 also where block column 0 lacks the row; otherwise list 0 equals list 1. `target_slots`: A filled slot of class c names in entry 0 a slot of its own row device and in entry 1 a slot of row device c modulo the number of row devices, within (c // number of row devices) * 2 and the 1 after it; both are filled or both -1, always -1 in classes 0 and 1; the target's block row number is at least its block column number. `diag_inverse`: each matrix is lower triangular.
All inputs are finite; a program needn't handle non-finite values.
Results may differ from the reference program's by a relative error of at most 0.0003.
Values sent between devices are 32-bit elements; how exact they have to be, the bound alone decides.
A program may use at most 128 MiB of HBM per device.

```python
import math
import jax
import jax.numpy as jnp
from jax import lax

BLOCK = 256
PER_CLASS = 2
GROUPS = 24
PANEL_SLOTS = 4
SLOTS = 8
N_ROW = 4
N_COL = 8


def structure(key):
    base_key = jax.random.fold_in(key, 17)
    member_keys = jax.random.split(jax.random.fold_in(base_key, 1), N_COL)
    members = jax.vmap(lambda member_key: jax.random.permutation(member_key, GROUPS)[:PER_CLASS])(member_keys).astype(jnp.int32)
    classes = jnp.arange(N_COL, dtype=jnp.int32)
    block_row = classes[:, None] + N_COL * members
    per_row = N_COL // N_ROW
    owner_class = jnp.arange(N_ROW, dtype=jnp.int32)[:, None] + N_ROW * jnp.arange(per_row, dtype=jnp.int32)[None, :]
    rows_panel = block_row[owner_class]
    valid_slot = (owner_class >= 2)[:, :, None]
    second_rows = jnp.where(valid_slot, rows_panel, -1).reshape(N_ROW, PANEL_SLOTS)
    kept_rows = jax.random.randint(jax.random.fold_in(base_key, 2), (N_ROW, PANEL_SLOTS), 0, 5) < 3
    first_rows = jnp.where(kept_rows & (second_rows >= 0), second_rows, -1)
    live_pairs = (second_rows[:, None, :, None] >= 0) & (second_rows[:, None, :, None] >= block_row[None, :, None, :]) & (classes >= 2)[None, :, None, None]
    live_pairs = live_pairs.reshape(N_ROW, N_COL, SLOTS)
    rank_keys = jax.random.split(jax.random.fold_in(base_key, 3), N_ROW * N_COL)
    rank_order = jax.vmap(lambda member_key: jax.random.permutation(member_key, SLOTS))(rank_keys).astype(jnp.int32).reshape(N_ROW, N_COL, SLOTS)
    scores = jnp.where(live_pairs, 0, SLOTS).astype(jnp.int32) + rank_order
    sort_order = jnp.argsort(scores, axis=-1, stable=True).astype(jnp.int32)
    chosen_live = jnp.take_along_axis(live_pairs, sort_order, axis=-1)
    row_slot = jnp.where(chosen_live, sort_order // PER_CLASS, -1)
    col_slot = jnp.where(chosen_live, (classes // N_ROW)[None, :, None] * PER_CLASS + sort_order % PER_CLASS, -1)
    target_table = jnp.stack([row_slot, col_slot]).transpose(0, 1, 3, 2).reshape(2, N_ROW * SLOTS, N_COL).astype(jnp.int32)
    panel_table = jnp.stack([first_rows, second_rows]).reshape(2, N_ROW * PANEL_SLOTS).astype(jnp.int32)
    return (panel_table, target_table)


def draw_panel_rows(key, part):
    return structure(key)[0]


def draw_target_slots(key, part):
    return structure(key)[1]


def draw_diag_inverse(key, part):
    base_key = jax.random.fold_in(key, 29)
    lower_key, diag_key = jax.random.split(base_key)
    block_shape = (2, BLOCK, BLOCK)
    lower = jax.random.normal(lower_key, block_shape, jnp.float32)
    diagonal = jax.random.uniform(diag_key, (2, BLOCK), jnp.float32, 0.5, 1.0)
    positions = jnp.arange(BLOCK)
    below = positions[:, None] > positions[None, :]
    on_diagonal = positions[:, None] == positions[None, :]
    return 0.3 * (jnp.where(below, lower * (0.8 / math.sqrt(BLOCK)), 0.0) + jnp.where(on_diagonal, diagonal[:, :, None], 0.0))


def block_levels(key, shape, pieces, low, top_value):
    factor_of = 1.0
    for position, parts in pieces:
        draws = jax.random.uniform(jax.random.fold_in(jax.random.fold_in(key, 6), position), (parts,), jnp.float32, low / len(pieces), top_value / len(pieces))
        factor_of = factor_of * jnp.repeat(jnp.exp(draws), shape[position] // parts).reshape((-1,) + (1,) * (len(shape) - 1 - position))
    return factor_of


def centred(rng, dims, width, bound, cuts=(), kind=jnp.bfloat16):
    values = width * jax.random.normal(rng, dims, jnp.float32)
    if cuts:
        values = values * block_levels(rng, dims, cuts, -0.22, 0.18)
    return jnp.clip(values, -bound, bound).astype(kind)


def setup_inputs(seed: int = 0) -> dict:
    keys = jax.random.split(jax.random.key(seed), 6)
    return {
        "blocks": centred(keys[0], (N_ROW * SLOTS, N_COL, BLOCK, BLOCK), 1.0, 6.0, ((0, 4), (1, 8)), jnp.float32),
        "panel_rows": draw_panel_rows(jax.random.fold_in(keys[5], 71), 0),
        "target_slots": draw_target_slots(jax.random.fold_in(keys[5], 71), 0),
        "diag_inverse": draw_diag_inverse(jax.random.fold_in(keys[5], 71), 0),
        "cross_block": centred(keys[4], (BLOCK, BLOCK), 1.0, 6.0, (), jnp.float32),
    }


HIGHEST_PRECISION = lax.Precision.HIGHEST


def reference(blocks, panel_rows, target_slots, diag_inverse, cross_block):
    block_grid = blocks.reshape(N_ROW, SLOTS, N_COL, BLOCK, BLOCK)
    first_live = (panel_rows[0] >= 0).reshape(N_ROW, PANEL_SLOTS)[:, :, None, None]
    second_live = (panel_rows[1] >= 0).reshape(N_ROW, PANEL_SLOTS)[:, :, None, None]
    cross_factor = jnp.dot(cross_block, diag_inverse[0].T, precision=HIGHEST_PRECISION)
    head_zero = block_grid[:, :PANEL_SLOTS, 0]
    head_one = block_grid[:, :PANEL_SLOTS, 1]
    first_factor = jnp.where(first_live, jnp.einsum("rsab,cb->rsac", head_zero, diag_inverse[0], precision=HIGHEST_PRECISION), 0.0)
    updated = head_one - jnp.einsum("rsab,cb->rsac", first_factor, cross_factor, precision=HIGHEST_PRECISION)
    second_factor = jnp.where(second_live, jnp.einsum("rsab,cb->rsac", updated, diag_inverse[1], precision=HIGHEST_PRECISION), 0.0)
    both_factors = jnp.concatenate([first_factor, second_factor], axis=3)
    slot_table = target_slots.reshape(2, N_ROW, SLOTS, N_COL)
    class_rows = jnp.arange(N_COL, dtype=jnp.int32) % N_ROW

    def one_row(device_row):
        row_index = slot_table[0, device_row]
        col_index = slot_table[1, device_row]
        present = row_index >= 0
        left_blocks = both_factors[device_row][jnp.where(present, row_index, 0)]
        right_blocks = both_factors[class_rows[None, :], jnp.where(present, col_index, 0)]
        schur_term = jnp.einsum("scak,scbk->scab", left_blocks, right_blocks, precision=HIGHEST_PRECISION)
        stored = block_grid[device_row]
        result = stored - jnp.where(present[:, :, None, None], schur_term, 0.0)
        result = result.at[:PANEL_SLOTS, 0].set(jnp.where(first_live[device_row], first_factor[device_row], result[:PANEL_SLOTS, 0]))
        result = result.at[:PANEL_SLOTS, 1].set(jnp.where(second_live[device_row], second_factor[device_row], result[:PANEL_SLOTS, 1]))
        return result

    factored = lax.map(one_row, jnp.arange(N_ROW, dtype=jnp.int32))
    return factored.reshape(blocks.shape)
```

```python
import functools

import jax
import jax.numpy as jnp
from jax import lax
from jax.experimental import pallas as pl
from jax.experimental.pallas import tpu as pltpu
from jax.sharding import PartitionSpec as P

PER_CLASS = 2
CHUNK = 64
MESH = pl.DeviceIdType.MESH
F32 = jnp.float32
BF16 = jnp.bfloat16
NN = (((1,), (0,)), ((), ()))
NT = (((1,), (1,)), ((), ()))


def split(x):
    high = x.astype(BF16)
    return high, (x - high.astype(F32)).astype(BF16)


def product(a, b, dims=NN):
    (ah, al), (bh, bl) = a, b
    dot = functools.partial(lax.dot_general, dimension_numbers=dims, preferred_element_type=F32)
    return dot(ah, bh) + (dot(ah, bl) + dot(al, bh))


def kernel(
    n_row, n_col, n_x,
    blocks, panel_rows, target_slots, diag_inverse, cross_block, out,
    own, left, right, terms, mixed_high, mixed_low,
    own_sem, left_recv, left_send, right_recv, right_send,
):
    n_y, n_z = n_row // 2, n_col // n_x
    slots, _, size, _ = blocks.shape
    panel = panel_rows.shape[1]
    pieces = size // CHUNK
    row, col = lax.axis_index("row"), lax.axis_index("col")
    y, core = lax.div(row, 2), lax.rem(row, 2)
    z, x = lax.div(col, n_x), lax.rem(col, n_x)

    def at(yy, cc, zz, xx):
        return (yy * 2 + cc, zz * n_x + xx)

    owner = lax.rem(col, n_row)
    owner_y, owner_core = lax.div(owner, 2), lax.rem(owner, 2)
    class_start = lax.div(col, n_row) * PER_CLASS
    has_targets = col >= 2
    holder = row == owner
    first_piece = jnp.where(row < 2, PER_CLASS * pieces, 0)

    for slot in range(slots):
        pltpu.make_async_copy(blocks.at[slot, 0], own.at[slot], own_sem.at[slot]).start()

    neighbours = (
        (z > 0, at(y, core, z - 1, x)),
        (z < n_z - 1, at(y, core, z + 1, x)),
        (x > 0, at(y, core, z, x - 1)),
        (x < n_x - 1, at(y, core, z, x + 1)),
        (y > 0, at(y - 1, core, z, x)),
        (y < n_y - 1, at(y + 1, core, z, x)),
        (row >= 0, at(y, 1 - core, z, x)),
    )
    barrier = pltpu.get_barrier_semaphore()
    expected = 0
    for exists, device in neighbours:
        @pl.when(exists)
        def _():
            pl.semaphore_signal(barrier, inc=1, device_id=device, device_id_type=MESH)
        expected = expected + jnp.where(exists, 1, 0)
    pl.semaphore_wait(barrier, expected)

    for slot in range(slots):
        pltpu.make_async_copy(blocks.at[slot, 0], own.at[slot], own_sem.at[slot]).wait()
    for stream in range(2):
        @pl.when(col == stream)
        def _():
            for slot in range(panel):
                live = jnp.full((size, size), panel_rows[stream, slot], jnp.int32) >= 0
                left[stream, slot] = jnp.where(live, own[slot], 0.0)

    def left_piece(stream, piece):
        rows = pl.ds(pl.multiple_of(lax.rem(piece, pieces) * CHUNK, CHUNK), CHUNK)
        return left.at[stream, lax.div(piece, pieces), rows]

    def right_piece(stream, piece):
        rows = pl.ds(pl.multiple_of(lax.rem(piece, pieces) * CHUNK, CHUNK), CHUNK)
        return right.at[stream, lax.div(piece, pieces), rows]

    def left_hops(stream):
        along_z = (x == stream) & (z < n_z - 1)
        up = (x >= stream) & (x < n_x - 1)
        down = (x <= stream) & (x > 0) & ((z > 0) | (x > 1))
        return (
            (along_z, at(y, core, z + 1, x)),
            (up, at(y, core, z, x + 1)),
            (down, at(y, core, z, x - 1)),
        )

    gets = (col != 0, (col != 0) & (col != 1))

    right_hops = (
        (has_targets & (core == owner_core) & (y >= owner_y) & (y < n_y - 1), at(y + 1, core, z, x)),
        (has_targets & (core == owner_core) & (y <= owner_y) & (y > 0), at(y - 1, core, z, x)),
        (has_targets & (core == owner_core), at(y, 1 - core, z, x)),
    )

    def left_copy(stream, hop, device, piece):
        part = left_piece(stream, piece)
        return pltpu.make_async_remote_copy(
            src_ref=part, dst_ref=part,
            send_sem=left_send.at[hop, stream, piece], recv_sem=left_recv.at[stream, piece],
            device_id=device, device_id_type=MESH,
        )

    def right_copy(source, stream, hop, device, piece):
        return pltpu.make_async_remote_copy(
            src_ref=source, dst_ref=right_piece(stream, piece),
            send_sem=right_send.at[hop, stream, piece], recv_sem=right_recv.at[stream, piece],
            device_id=device, device_id_type=MESH,
        )

    def left_step(piece, carry):
        for stream in range(2):
            @pl.when(gets[stream])
            def _():
                left_copy(stream, 0, (row, col), piece).wait_recv()
            for hop, (wanted, device) in enumerate(left_hops(stream)):
                @pl.when(wanted)
                def _():
                    left_copy(stream, hop, device, piece).start()

        owned = piece - class_start * pieces
        @pl.when(has_targets & holder & (owned >= 0) & (owned < PER_CLASS * pieces))
        def _():
            for stream in range(2):
                for hop, (wanted, device) in enumerate(right_hops):
                    @pl.when(wanted)
                    def _():
                        right_copy(left_piece(stream, piece), stream, hop, device, owned).start()

        arriving = piece - (panel - PER_CLASS) * pieces
        @pl.when(has_targets & jnp.logical_not(holder) & (arriving >= 0))
        def _():
            for stream in range(2):
                part = right_piece(stream, arriving)
                right_copy(part, stream, 0, (row, col), arriving).wait_recv()
                for hop, (wanted, device) in enumerate(right_hops):
                    @pl.when(wanted)
                    def _():
                        right_copy(part, stream, hop, device, arriving).start()
        return carry

    lax.fori_loop(first_piece, panel * pieces, left_step, 0)

    inverse0, inverse1 = split(diag_inverse[0]), split(diag_inverse[1])
    cross = product(split(cross_block[...]), inverse0, NT)
    cross_parts = split(cross)

    @pl.when(col == 0)
    def _():
        for slot in range(panel):
            live = jnp.full((size, size), panel_rows[0, slot], jnp.int32) >= 0
            first = product(split(left[0, slot]), inverse0, NT)
            out[slot, 0] = jnp.where(live, first, own[slot])
        for slot in range(panel, slots):
            out[slot, 0] = own[slot]

    @pl.when(col == 1)
    def _():
        for slot in range(panel):
            live = jnp.full((size, size), panel_rows[1, slot], jnp.int32) >= 0
            body = own[slot]

            def second_of():
                first = product(split(left[0, slot]), inverse0, NT)
                updated = body - product(split(first), cross_parts, NT)
                return product(split(updated), inverse1, NT)

            if slot < PER_CLASS:
                @pl.when(row < 2)
                def _():
                    out[slot, 0] = body

                @pl.when(row >= 2)
                def _():
                    out[slot, 0] = jnp.where(live, second_of(), body)
            else:
                out[slot, 0] = jnp.where(live, second_of(), body)
        for slot in range(panel, slots):
            out[slot, 0] = own[slot]

    @pl.when(has_targets)
    def _():
        @pl.when(holder)
        def _():
            for stream in range(2):
                for m in range(PER_CLASS):
                    right[stream, m] = left[stream, class_start + m]

        inverse0_t, inverse1_t = split(diag_inverse[0].T), split(diag_inverse[1].T)
        cross_t = split(cross.T)
        wide = PER_CLASS * size
        first_t = product(inverse0, split(right[0].reshape(wide, size)), NT)
        second_t = product(inverse1, split(right[1].reshape(wide, size)), NT) - product(
            inverse1, split(product(cross_parts, split(first_t)))
        )
        upper = product(inverse1_t, split(second_t))
        lower = product(inverse0_t, split(first_t - product(cross_t, split(upper))))
        for place, part in ((0, lower), (size, upper)):
            high, low = split(part)
            mixed_high[place:place + size, :] = high
            mixed_low[place:place + size, :] = low

        def slot_step(slot, carry):
            both = jnp.concatenate([left[0, slot], left[1, slot]], axis=1)
            term = product(split(both), (mixed_high[...], mixed_low[...]))
            for m in range(PER_CLASS):
                terms[slot * PER_CLASS + m] = term[:, m * size:(m + 1) * size]
            return carry

        lax.fori_loop(lax.div(first_piece, pieces), panel, slot_step, 0)

        @pl.when(row < 2)
        def _():
            for slot in range(PER_CLASS * PER_CLASS):
                terms[slot] = jnp.zeros((size, size), F32)

        for slot in range(slots):
            row_index = target_slots[0, slot, 0]
            col_index = target_slots[1, slot, 0]
            place = jnp.where(
                row_index >= 0,
                row_index * PER_CLASS + jnp.clip(col_index - class_start, 0, PER_CLASS - 1),
                0,
            )
            present = jnp.full((size, size), row_index, jnp.int32) >= 0
            out[slot, 0] = own[slot] - jnp.where(present, terms[place], 0.0)

    def drain(piece, carry):
        for stream in range(2):
            for hop, (wanted, device) in enumerate(left_hops(stream)):
                @pl.when(wanted)
                def _():
                    left_copy(stream, hop, device, piece).wait_send()
        return carry

    lax.fori_loop(first_piece, panel * pieces, drain, 0)

    def drain_right(piece, carry):
        for stream in range(2):
            for hop, (wanted, device) in enumerate(right_hops):
                @pl.when(wanted)
                def _():
                    part = right_piece(stream, piece)
                    right_copy(part, stream, hop, device, piece).wait_send()
        return carry

    lax.fori_loop(0, PER_CLASS * pieces, drain_right, 0)


def per_device(n_row, n_col, n_x, blocks, panel_rows, target_slots, diag_inverse, cross_block):
    slots, _, size, _ = blocks.shape
    panel = panel_rows.shape[1]
    count = panel * (size // CHUNK)
    right_count = PER_CLASS * (size // CHUNK)
    vmem = pl.BlockSpec(memory_space=pltpu.VMEM)
    smem = pl.BlockSpec(memory_space=pltpu.SMEM)
    return pl.pallas_call(
        functools.partial(kernel, n_row, n_col, n_x),
        out_shape=jax.ShapeDtypeStruct(blocks.shape, blocks.dtype),
        in_specs=[pl.BlockSpec(memory_space=pl.ANY), smem, smem, vmem, vmem],
        out_specs=vmem,
        scratch_shapes=[
            pltpu.VMEM((slots, size, size), F32),
            pltpu.VMEM((2, panel, size, size), F32),
            pltpu.VMEM((2, PER_CLASS, size, size), F32),
            pltpu.VMEM((panel * PER_CLASS, size, size), F32),
            pltpu.VMEM((2 * size, PER_CLASS * size), BF16),
            pltpu.VMEM((2 * size, PER_CLASS * size), BF16),
            pltpu.SemaphoreType.DMA((slots,)),
            pltpu.SemaphoreType.DMA((2, count)),
            pltpu.SemaphoreType.DMA((3, 2, count)),
            pltpu.SemaphoreType.DMA((2, right_count)),
            pltpu.SemaphoreType.DMA((3, 2, right_count)),
        ],
        compiler_params=pltpu.CompilerParams(
            collective_id=0, has_side_effects=True, vmem_limit_bytes=48 * 2**20
        ),
        cost_estimate=pl.CostEstimate(
            flops=2 * size**3 * 34 * 3, bytes_accessed=8 * slots * size * size, transcendentals=0
        ),
    )(blocks, panel_rows, target_slots, diag_inverse, cross_block)


def solution(mesh):
    n_row, n_col = mesh.shape["row"], mesh.shape["col"]
    n_x = n_row // 2
    return jax.shard_map(
        functools.partial(per_device, n_row, n_col, n_x),
        mesh=mesh,
        in_specs=(P("row", "col", None, None), P(None, "row"), P(None, "row", "col"), P(), P()),
        out_specs=P("row", "col", None, None),
        check_vma=False,
    )
```

```python
import functools

import jax
import jax.numpy as jnp
from jax import lax
from jax.experimental import pallas as pl
from jax.experimental.pallas import tpu as pltpu
from jax.sharding import PartitionSpec as P

PER_CLASS = 2
CHUNK = 64
MESH = pl.DeviceIdType.MESH
F32 = jnp.float32
BF16 = jnp.bfloat16
NN = (((1,), (0,)), ((), ()))
NT = (((1,), (1,)), ((), ()))


def split(x):
    high = x.astype(BF16)
    return high, (x - high.astype(F32)).astype(BF16)


def product(a, b, dims=NN):
    (ah, al), (bh, bl) = a, b
    dot = functools.partial(lax.dot_general, dimension_numbers=dims, preferred_element_type=F32)
    return dot(ah, bh) + (dot(ah, bl) + dot(al, bh))


def kernel(
    n_row, n_col, n_x,
    blocks, panel_rows, target_slots, inverse_in, cross_in, out,
    diag_inverse, cross_block, own, left, right, terms, mixed_high, mixed_low,
    given_sem, own_sem, left_recv, left_send, right_recv, right_send,
):
    n_y, n_z = n_row // 2, n_col // n_x
    slots, _, size, _ = blocks.shape
    panel = panel_rows.shape[1]
    pieces = size // CHUNK
    row, col = lax.axis_index("row"), lax.axis_index("col")
    y, core = lax.div(row, 2), lax.rem(row, 2)
    z, x = lax.div(col, n_x), lax.rem(col, n_x)

    def at(yy, cc, zz, xx):
        return (yy * 2 + cc, zz * n_x + xx)

    owner = lax.rem(col, n_row)
    owner_y, owner_core = lax.div(owner, 2), lax.rem(owner, 2)
    class_start = lax.div(col, n_row) * PER_CLASS
    has_targets = col >= 2
    holder = row == owner
    first_piece = jnp.where(row < 2, PER_CLASS * pieces, 0)

    for slot in range(slots):
        pltpu.make_async_copy(blocks.at[slot, 0], own.at[slot], own_sem.at[slot]).start()

    given = (
        pltpu.make_async_copy(inverse_in, diag_inverse, given_sem.at[0]),
        pltpu.make_async_copy(cross_in, cross_block, given_sem.at[1]),
    )
    for copy in given:
        copy.start()

    neighbours = (
        (z > 0, at(y, core, z - 1, x)),
        (z < n_z - 1, at(y, core, z + 1, x)),
        (x > 0, at(y, core, z, x - 1)),
        (x < n_x - 1, at(y, core, z, x + 1)),
        (y > 0, at(y - 1, core, z, x)),
        (y < n_y - 1, at(y + 1, core, z, x)),
        (y > 0, at(y - 1, 1 - core, z, x)),
        (y < n_y - 1, at(y + 1, 1 - core, z, x)),
    )
    barrier = pltpu.get_barrier_semaphore()
    expected = 0
    for exists, device in neighbours:
        @pl.when(exists)
        def _():
            pl.semaphore_signal(barrier, inc=1, device_id=device, device_id_type=MESH)
        expected = expected + jnp.where(exists, 1, 0)
    pl.semaphore_wait(barrier, expected)

    for slot in range(slots):
        pltpu.make_async_copy(blocks.at[slot, 0], own.at[slot], own_sem.at[slot]).wait()
    for stream in range(2):
        @pl.when(col == stream)
        def _():
            for slot in range(panel):
                live = jnp.full((size, size), panel_rows[stream, slot], jnp.int32) >= 0
                left[stream, slot] = jnp.where(live, own[slot], 0.0)

    def left_piece(stream, piece):
        rows = pl.ds(pl.multiple_of(lax.rem(piece, pieces) * CHUNK, CHUNK), CHUNK)
        return left.at[stream, lax.div(piece, pieces), rows]

    def right_piece(stream, piece):
        rows = pl.ds(pl.multiple_of(lax.rem(piece, pieces) * CHUNK, CHUNK), CHUNK)
        return right.at[stream, lax.div(piece, pieces), rows]

    def left_hops(stream):
        along_z = (x == stream) & (z < n_z - 1)
        up = (x >= stream) & (x < n_x - 1)
        down = (x <= stream) & (x > 0) & ((z > 0) | (x > 1))
        return (
            (along_z, at(y, core, z + 1, x)),
            (up, at(y, core, z, x + 1)),
            (down, at(y, core, z, x - 1)),
        )

    gets = (col != 0, (col != 0) & (col != 1))

    same, before, after = core == owner_core, y < owner_y, y > owner_y
    up = (same & jnp.logical_not(before)) | (jnp.logical_not(same) & after)
    up = up | (jnp.logical_not(same) & (y == owner_y - 1) & (owner_y == n_y - 1))
    down = (same & jnp.logical_not(after)) | (jnp.logical_not(same) & before)
    down = down | (jnp.logical_not(same) & (y == owner_y + 1))
    right_hops = (
        (has_targets & up & (y < n_y - 1), at(y + 1, core, z, x)),
        (has_targets & down & (y > 0), at(y - 1, core, z, x)),
        (has_targets & holder & (y < n_y - 1), at(y + 1, 1 - core, z, x)),
        (has_targets & holder & (y > 0), at(y - 1, 1 - core, z, x)),
    )

    def left_copy(stream, hop, device, piece):
        part = left_piece(stream, piece)
        return pltpu.make_async_remote_copy(
            src_ref=part, dst_ref=part,
            send_sem=left_send.at[hop, stream, piece], recv_sem=left_recv.at[stream, piece],
            device_id=device, device_id_type=MESH,
        )

    def right_copy(source, stream, hop, device, piece):
        return pltpu.make_async_remote_copy(
            src_ref=source, dst_ref=right_piece(stream, piece),
            send_sem=right_send.at[hop, stream, piece], recv_sem=right_recv.at[stream, piece],
            device_id=device, device_id_type=MESH,
        )

    def left_step(piece):
        for stream in range(2):
            @pl.when(gets[stream])
            def _():
                left_copy(stream, 0, (row, col), piece).wait_recv()
            for hop, (wanted, device) in enumerate(left_hops(stream)):
                @pl.when(wanted)
                def _():
                    left_copy(stream, hop, device, piece).start()

        owned = piece - class_start * pieces
        @pl.when(has_targets & holder & (owned >= 0) & (owned < PER_CLASS * pieces))
        def _():
            for stream in range(2):
                for hop, (wanted, device) in enumerate(right_hops):
                    @pl.when(wanted)
                    def _():
                        right_copy(left_piece(stream, piece), stream, hop, device, owned).start()

    def right_step(arriving):
        for stream in range(2):
            part = right_piece(stream, arriving)
            right_copy(part, stream, 0, (row, col), arriving).wait_recv()
            for hop, (wanted, device) in enumerate(right_hops[:2]):
                @pl.when(wanted)
                def _():
                    right_copy(part, stream, hop, device, arriving).start()

    right_start = jnp.where(row < 2, panel * pieces, (panel - PER_CLASS) * pieces)

    def step(piece, carry):
        @pl.when(piece < panel * pieces)
        def _():
            left_step(piece)

        @pl.when(has_targets & jnp.logical_not(holder) & (piece >= right_start))
        def _():
            right_step(piece - right_start)
        return carry

    lax.fori_loop(first_piece, right_start + PER_CLASS * pieces, step, 0)

    for copy in given:
        copy.wait()
    inverse0, inverse1 = split(diag_inverse[0]), split(diag_inverse[1])
    cross = product(split(cross_block[...]), inverse0, NT)
    cross_parts = split(cross)

    @pl.when(col == 0)
    def _():
        for slot in range(panel):
            live = jnp.full((size, size), panel_rows[0, slot], jnp.int32) >= 0
            first = product(split(left[0, slot]), inverse0, NT)
            out[slot, 0] = jnp.where(live, first, own[slot])
        for slot in range(panel, slots):
            out[slot, 0] = own[slot]

    @pl.when(col == 1)
    def _():
        for slot in range(panel):
            live = jnp.full((size, size), panel_rows[1, slot], jnp.int32) >= 0
            body = own[slot]

            def second_of():
                first = product(split(left[0, slot]), inverse0, NT)
                updated = body - product(split(first), cross_parts, NT)
                return product(split(updated), inverse1, NT)

            if slot < PER_CLASS:
                @pl.when(row < 2)
                def _():
                    out[slot, 0] = body

                @pl.when(row >= 2)
                def _():
                    out[slot, 0] = jnp.where(live, second_of(), body)
            else:
                out[slot, 0] = jnp.where(live, second_of(), body)
        for slot in range(panel, slots):
            out[slot, 0] = own[slot]

    @pl.when(has_targets)
    def _():
        @pl.when(holder)
        def _():
            for stream in range(2):
                for m in range(PER_CLASS):
                    right[stream, m] = left[stream, class_start + m]

        inverse0_t, inverse1_t = split(diag_inverse[0].T), split(diag_inverse[1].T)
        cross_t = split(cross.T)
        wide = PER_CLASS * size
        first_t = product(inverse0, split(right[0].reshape(wide, size)), NT)
        second_t = product(inverse1, split(right[1].reshape(wide, size)), NT) - product(
            inverse1, split(product(cross_parts, split(first_t)))
        )
        upper = product(inverse1_t, split(second_t))
        lower = product(inverse0_t, split(first_t - product(cross_t, split(upper))))
        for place, part in ((0, lower), (size, upper)):
            high, low = split(part)
            mixed_high[place:place + size, :] = high
            mixed_low[place:place + size, :] = low

        def slot_step(slot, carry):
            both = jnp.concatenate([left[0, slot], left[1, slot]], axis=1)
            term = product(split(both), (mixed_high[...], mixed_low[...]))
            for m in range(PER_CLASS):
                terms[slot * PER_CLASS + m] = term[:, m * size:(m + 1) * size]
            return carry

        lax.fori_loop(lax.div(first_piece, pieces), panel, slot_step, 0)

        @pl.when(row < 2)
        def _():
            for slot in range(PER_CLASS * PER_CLASS):
                terms[slot] = jnp.zeros((size, size), F32)

        for slot in range(slots):
            row_index = target_slots[0, slot, 0]
            col_index = target_slots[1, slot, 0]
            place = jnp.where(
                row_index >= 0,
                row_index * PER_CLASS + jnp.clip(col_index - class_start, 0, PER_CLASS - 1),
                0,
            )
            present = jnp.full((size, size), row_index, jnp.int32) >= 0
            out[slot, 0] = own[slot] - jnp.where(present, terms[place], 0.0)

    def drain(piece, carry):
        for stream in range(2):
            for hop, (wanted, device) in enumerate(left_hops(stream)):
                @pl.when(wanted)
                def _():
                    left_copy(stream, hop, device, piece).wait_send()
        return carry

    lax.fori_loop(first_piece, panel * pieces, drain, 0)

    def drain_right(piece, carry):
        for stream in range(2):
            for hop, (wanted, device) in enumerate(right_hops):
                @pl.when(wanted)
                def _():
                    part = right_piece(stream, piece)
                    right_copy(part, stream, hop, device, piece).wait_send()
        return carry

    lax.fori_loop(0, PER_CLASS * pieces, drain_right, 0)


def per_device(n_row, n_col, n_x, blocks, panel_rows, target_slots, diag_inverse, cross_block):
    slots, _, size, _ = blocks.shape
    panel = panel_rows.shape[1]
    count = panel * (size // CHUNK)
    right_count = PER_CLASS * (size // CHUNK)
    vmem = pl.BlockSpec(memory_space=pltpu.VMEM)
    anywhere = pl.BlockSpec(memory_space=pl.ANY)
    smem = pl.BlockSpec(memory_space=pltpu.SMEM)
    return pl.pallas_call(
        functools.partial(kernel, n_row, n_col, n_x),
        out_shape=jax.ShapeDtypeStruct(blocks.shape, blocks.dtype),
        in_specs=[anywhere, smem, smem, anywhere, anywhere],
        out_specs=vmem,
        scratch_shapes=[
            pltpu.VMEM(diag_inverse.shape, F32),
            pltpu.VMEM(cross_block.shape, F32),
            pltpu.VMEM((slots, size, size), F32),
            pltpu.VMEM((2, panel, size, size), F32),
            pltpu.VMEM((2, PER_CLASS, size, size), F32),
            pltpu.VMEM((panel * PER_CLASS, size, size), F32),
            pltpu.VMEM((2 * size, PER_CLASS * size), BF16),
            pltpu.VMEM((2 * size, PER_CLASS * size), BF16),
            pltpu.SemaphoreType.DMA((2,)),
            pltpu.SemaphoreType.DMA((slots,)),
            pltpu.SemaphoreType.DMA((2, count)),
            pltpu.SemaphoreType.DMA((3, 2, count)),
            pltpu.SemaphoreType.DMA((2, right_count)),
            pltpu.SemaphoreType.DMA((4, 2, right_count)),
        ],
        compiler_params=pltpu.CompilerParams(
            collective_id=0, has_side_effects=True, vmem_limit_bytes=48 * 2**20
        ),
        cost_estimate=pl.CostEstimate(
            flops=2 * size**3 * 34 * 3, bytes_accessed=8 * slots * size * size, transcendentals=0
        ),
    )(blocks, panel_rows, target_slots, diag_inverse, cross_block)


def solution(mesh):
    n_row, n_col = mesh.shape["row"], mesh.shape["col"]
    n_x = n_row // 2
    return jax.shard_map(
        functools.partial(per_device, n_row, n_col, n_x),
        mesh=mesh,
        in_specs=(P("row", "col", None, None), P(None, "row"), P(None, "row", "col"), P(), P()),
        out_specs=P("row", "col", None, None),
        check_vma=False,
    )
```

```python
import functools

import jax
import jax.numpy as jnp
from jax import lax
from jax.experimental import pallas as pl
from jax.experimental.pallas import tpu as pltpu
from jax.sharding import PartitionSpec as P

PER_CLASS = 2
CHUNK = 64
LAG = 3
MESH = pl.DeviceIdType.MESH
F32 = jnp.float32
BF16 = jnp.bfloat16
NN = (((1,), (0,)), ((), ()))
NT = (((1,), (1,)), ((), ()))


def split(x):
    high = x.astype(BF16)
    return high, (x - high.astype(F32)).astype(BF16)


def product(a, b, dims=NN):
    (ah, al), (bh, bl) = a, b
    dot = functools.partial(lax.dot_general, dimension_numbers=dims, preferred_element_type=F32)
    return dot(ah, bh) + (dot(ah, bl) + dot(al, bh))


def kernel(
    n_row, n_col, n_x,
    blocks, panel_rows, target_slots, inverse_in, cross_in, out,
    diag_inverse, cross_block, own, left, right, terms, mixed_high, mixed_low,
    given_sem, own_sem, left_recv, left_send, right_recv, right_send,
):
    n_y, n_z = n_row // 2, n_col // n_x
    slots, _, size, _ = blocks.shape
    panel = panel_rows.shape[1]
    pieces = size // CHUNK
    row, col = lax.axis_index("row"), lax.axis_index("col")
    y, core = lax.div(row, 2), lax.rem(row, 2)
    z, x = lax.div(col, n_x), lax.rem(col, n_x)

    def at(yy, cc, zz, xx):
        return (yy * 2 + cc, zz * n_x + xx)

    owner = lax.rem(col, n_row)
    owner_y, owner_core = lax.div(owner, 2), lax.rem(owner, 2)
    class_start = lax.div(col, n_row) * PER_CLASS
    has_targets = col >= 2
    holder = row == owner
    first_piece = jnp.where(row < 2, PER_CLASS * pieces, 0)

    for slot in range(slots):
        pltpu.make_async_copy(blocks.at[slot, 0], own.at[slot], own_sem.at[slot]).start()

    given = (
        pltpu.make_async_copy(inverse_in, diag_inverse, given_sem.at[0]),
        pltpu.make_async_copy(cross_in, cross_block, given_sem.at[1]),
    )
    for copy in given:
        copy.start()

    neighbours = (
        (z > 0, at(y, core, z - 1, x)),
        (z < n_z - 1, at(y, core, z + 1, x)),
        (x > 0, at(y, core, z, x - 1)),
        (x < n_x - 1, at(y, core, z, x + 1)),
        (y > 0, at(y - 1, core, z, x)),
        (y < n_y - 1, at(y + 1, core, z, x)),
        (y > 0, at(y - 1, 1 - core, z, x)),
        (y < n_y - 1, at(y + 1, 1 - core, z, x)),
    )
    barrier = pltpu.get_barrier_semaphore()
    expected = 0
    for exists, device in neighbours:
        @pl.when(exists)
        def _():
            pl.semaphore_signal(barrier, inc=1, device_id=device, device_id_type=MESH)
        expected = expected + jnp.where(exists, 1, 0)
    pl.semaphore_wait(barrier, expected)

    for slot in range(slots):
        pltpu.make_async_copy(blocks.at[slot, 0], own.at[slot], own_sem.at[slot]).wait()
    for stream in range(2):
        @pl.when(col == stream)
        def _():
            for slot in range(panel):
                live = jnp.full((size, size), panel_rows[stream, slot], jnp.int32) >= 0
                left[stream, slot] = jnp.where(live, own[slot], 0.0)

    def left_piece(stream, piece):
        rows = pl.ds(pl.multiple_of(lax.rem(piece, pieces) * CHUNK, CHUNK), CHUNK)
        return left.at[stream, lax.div(piece, pieces), rows]

    def right_piece(stream, piece):
        rows = pl.ds(pl.multiple_of(lax.rem(piece, pieces) * CHUNK, CHUNK), CHUNK)
        return right.at[stream, lax.div(piece, pieces), rows]

    def left_hops(stream):
        along_z = (x == stream) & (z < n_z - 1)
        up = (x >= stream) & (x < n_x - 1)
        down = (x <= stream) & (x > 0) & ((z > 0) | (x > 1))
        return (
            (along_z, at(y, core, z + 1, x)),
            (up, at(y, core, z, x + 1)),
            (down, at(y, core, z, x - 1)),
        )

    gets = (col != 0, (col != 0) & (col != 1))

    same, before, after = core == owner_core, y < owner_y, y > owner_y
    up = (same & jnp.logical_not(before)) | (jnp.logical_not(same) & after)
    up = up | (jnp.logical_not(same) & (y == owner_y - 1) & (owner_y == n_y - 1))
    down = (same & jnp.logical_not(after)) | (jnp.logical_not(same) & before)
    down = down | (jnp.logical_not(same) & (y == owner_y + 1))
    right_hops = (
        (has_targets & up & (y < n_y - 1), at(y + 1, core, z, x)),
        (has_targets & down & (y > 0), at(y - 1, core, z, x)),
        (has_targets & holder & (y < n_y - 1), at(y + 1, 1 - core, z, x)),
        (has_targets & holder & (y > 0), at(y - 1, 1 - core, z, x)),
    )

    def left_copy(stream, hop, device, piece):
        part = left_piece(stream, piece)
        return pltpu.make_async_remote_copy(
            src_ref=part, dst_ref=part,
            send_sem=left_send.at[hop, stream, piece], recv_sem=left_recv.at[stream, piece],
            device_id=device, device_id_type=MESH,
        )

    def right_copy(source, stream, hop, device, piece):
        return pltpu.make_async_remote_copy(
            src_ref=source, dst_ref=right_piece(stream, piece),
            send_sem=right_send.at[hop, stream, piece], recv_sem=right_recv.at[stream, piece],
            device_id=device, device_id_type=MESH,
        )

    def left_step(stream, piece):
        @pl.when(gets[stream])
        def _():
            left_copy(stream, 0, (row, col), piece).wait_recv()
        for hop, (wanted, device) in enumerate(left_hops(stream)):
            @pl.when(wanted)
            def _():
                left_copy(stream, hop, device, piece).start()

        owned = piece - class_start * pieces
        @pl.when(has_targets & holder & (owned >= 0) & (owned < PER_CLASS * pieces))
        def _():
            for hop, (wanted, device) in enumerate(right_hops):
                @pl.when(wanted)
                def _():
                    right_copy(left_piece(stream, piece), stream, hop, device, owned).start()

    def right_step(arriving):
        for stream in range(2):
            part = right_piece(stream, arriving)
            right_copy(part, stream, 0, (row, col), arriving).wait_recv()
            for hop, (wanted, device) in enumerate(right_hops[:2]):
                @pl.when(wanted)
                def _():
                    right_copy(part, stream, hop, device, arriving).start()

    longest = LAG * (n_x - 1)
    right_start = jnp.where(
        row < 2, panel * pieces + longest, (panel - PER_CLASS) * pieces + longest + 5
    )

    def step(piece, carry):
        for stream in range(2):
            lagged = piece - LAG * jnp.abs(x - stream)
            @pl.when((lagged >= first_piece) & (lagged < panel * pieces))
            def _():
                left_step(stream, lagged)

        @pl.when(has_targets & jnp.logical_not(holder) & (piece >= right_start) & (piece < right_start + PER_CLASS * pieces))
        def _():
            right_step(piece - right_start)
        return carry

    lax.fori_loop(first_piece, jnp.maximum(right_start + PER_CLASS * pieces, panel * pieces + longest), step, 0)

    for copy in given:
        copy.wait()
    inverse0, inverse1 = split(diag_inverse[0]), split(diag_inverse[1])
    cross = product(split(cross_block[...]), inverse0, NT)
    cross_parts = split(cross)

    @pl.when(col == 0)
    def _():
        for slot in range(panel):
            live = jnp.full((size, size), panel_rows[0, slot], jnp.int32) >= 0
            first = product(split(left[0, slot]), inverse0, NT)
            out[slot, 0] = jnp.where(live, first, own[slot])
        for slot in range(panel, slots):
            out[slot, 0] = own[slot]

    @pl.when(col == 1)
    def _():
        for slot in range(panel):
            live = jnp.full((size, size), panel_rows[1, slot], jnp.int32) >= 0
            body = own[slot]

            def second_of():
                first = product(split(left[0, slot]), inverse0, NT)
                updated = body - product(split(first), cross_parts, NT)
                return product(split(updated), inverse1, NT)

            if slot < PER_CLASS:
                @pl.when(row < 2)
                def _():
                    out[slot, 0] = body

                @pl.when(row >= 2)
                def _():
                    out[slot, 0] = jnp.where(live, second_of(), body)
            else:
                out[slot, 0] = jnp.where(live, second_of(), body)
        for slot in range(panel, slots):
            out[slot, 0] = own[slot]

    @pl.when(has_targets)
    def _():
        @pl.when(holder)
        def _():
            for stream in range(2):
                for m in range(PER_CLASS):
                    right[stream, m] = left[stream, class_start + m]

        inverse0_t, inverse1_t = split(diag_inverse[0].T), split(diag_inverse[1].T)
        cross_t = split(cross.T)
        wide = PER_CLASS * size
        first_t = product(inverse0, split(right[0].reshape(wide, size)), NT)
        second_t = product(inverse1, split(right[1].reshape(wide, size)), NT) - product(
            inverse1, split(product(cross_parts, split(first_t)))
        )
        upper = product(inverse1_t, split(second_t))
        lower = product(inverse0_t, split(first_t - product(cross_t, split(upper))))
        for place, part in ((0, lower), (size, upper)):
            high, low = split(part)
            mixed_high[place:place + size, :] = high
            mixed_low[place:place + size, :] = low

        def slot_step(slot, carry):
            both = jnp.concatenate([left[0, slot], left[1, slot]], axis=1)
            term = product(split(both), (mixed_high[...], mixed_low[...]))
            for m in range(PER_CLASS):
                terms[slot * PER_CLASS + m] = term[:, m * size:(m + 1) * size]
            return carry

        lax.fori_loop(lax.div(first_piece, pieces), panel, slot_step, 0)

        @pl.when(row < 2)
        def _():
            for slot in range(PER_CLASS * PER_CLASS):
                terms[slot] = jnp.zeros((size, size), F32)

        for slot in range(slots):
            row_index = target_slots[0, slot, 0]
            col_index = target_slots[1, slot, 0]
            place = jnp.where(
                row_index >= 0,
                row_index * PER_CLASS + jnp.clip(col_index - class_start, 0, PER_CLASS - 1),
                0,
            )
            present = jnp.full((size, size), row_index, jnp.int32) >= 0
            out[slot, 0] = own[slot] - jnp.where(present, terms[place], 0.0)

    def drain(piece, carry):
        for stream in range(2):
            for hop, (wanted, device) in enumerate(left_hops(stream)):
                @pl.when(wanted)
                def _():
                    left_copy(stream, hop, device, piece).wait_send()
        return carry

    lax.fori_loop(first_piece, panel * pieces, drain, 0)

    def drain_right(piece, carry):
        for stream in range(2):
            for hop, (wanted, device) in enumerate(right_hops):
                @pl.when(wanted)
                def _():
                    part = right_piece(stream, piece)
                    right_copy(part, stream, hop, device, piece).wait_send()
        return carry

    lax.fori_loop(0, PER_CLASS * pieces, drain_right, 0)


def per_device(n_row, n_col, n_x, blocks, panel_rows, target_slots, diag_inverse, cross_block):
    slots, _, size, _ = blocks.shape
    panel = panel_rows.shape[1]
    count = panel * (size // CHUNK)
    right_count = PER_CLASS * (size // CHUNK)
    vmem = pl.BlockSpec(memory_space=pltpu.VMEM)
    anywhere = pl.BlockSpec(memory_space=pl.ANY)
    smem = pl.BlockSpec(memory_space=pltpu.SMEM)
    return pl.pallas_call(
        functools.partial(kernel, n_row, n_col, n_x),
        out_shape=jax.ShapeDtypeStruct(blocks.shape, blocks.dtype),
        in_specs=[anywhere, smem, smem, anywhere, anywhere],
        out_specs=vmem,
        scratch_shapes=[
            pltpu.VMEM(diag_inverse.shape, F32),
            pltpu.VMEM(cross_block.shape, F32),
            pltpu.VMEM((slots, size, size), F32),
            pltpu.VMEM((2, panel, size, size), F32),
            pltpu.VMEM((2, PER_CLASS, size, size), F32),
            pltpu.VMEM((panel * PER_CLASS, size, size), F32),
            pltpu.VMEM((2 * size, PER_CLASS * size), BF16),
            pltpu.VMEM((2 * size, PER_CLASS * size), BF16),
            pltpu.SemaphoreType.DMA((2,)),
            pltpu.SemaphoreType.DMA((slots,)),
            pltpu.SemaphoreType.DMA((2, count)),
            pltpu.SemaphoreType.DMA((3, 2, count)),
            pltpu.SemaphoreType.DMA((2, right_count)),
            pltpu.SemaphoreType.DMA((4, 2, right_count)),
        ],
        compiler_params=pltpu.CompilerParams(
            collective_id=0, has_side_effects=True, vmem_limit_bytes=48 * 2**20
        ),
        cost_estimate=pl.CostEstimate(
            flops=2 * size**3 * 34 * 3, bytes_accessed=8 * slots * size * size, transcendentals=0
        ),
    )(blocks, panel_rows, target_slots, diag_inverse, cross_block)


def solution(mesh):
    n_row, n_col = mesh.shape["row"], mesh.shape["col"]
    n_x = n_row // 2
    return jax.shard_map(
        functools.partial(per_device, n_row, n_col, n_x),
        mesh=mesh,
        in_specs=(P("row", "col", None, None), P(None, "row"), P(None, "row", "col"), P(), P()),
        out_specs=P("row", "col", None, None),
        check_vma=False,
    )
```
